1024 devices in a mesh: row: 64 (over z, y_hi, core), col: 16 (over y_lo, x).
Axes of the slice: x: 8, y: 8 (y_hi: 4, y_lo: 2; y = y_hi * 2 + y_lo), z: 8, core: 2. Of those that a mesh axis runs over, the one named last changes fastest.
Arguments:
- pair_elems: bfloat16 [1024, 2, 20480], P(('row', 'col')), may hold values from -3.171875 to 3.171875
- slot_pair: int32 [1024], replicated, may hold values from 0 to 1023, each once
- val_index: int32 [1024], replicated, may hold values from 0 to 2047
- cond_index: int32 [1024], replicated, may hold values from 0 to 2047
- val_energy: float32 [2048], replicated, may hold values from -12 to -1
- cond_energy: float32 [2048], replicated, may hold values from 0.5 to 10
Outputs:
- chi_zero: float32 [2, 20480, 20480], P(None, 'row', 'col')
The draws below stay inside these ranges and needn't reach their ends.
Inputs may be any that keep to these rules, and one draw needn't show every extreme that they name: `slot_pair`: each pair is held by exactly one slot.
All inputs are finite; a program needn't handle non-finite values.
Results may differ from the reference program's by a relative error of at most 0.0028.
Values may be sent and summed in bfloat16 or wider, within the bound.
No kernel may reach another device: no remote copies, remote signals or barrier semaphores. Data moves between devices by JAX's collectives and lax.ppermute only.
A program may use at most 64 MiB of HBM per device.

```python
import jax
import jax.numpy as jnp
from jax import lax

NPW = 20480
NVAL = 2048
NCOND = 2048
PAIRS = 1024


def plant(values, key, smallest, largest):
    longest = values.shape.index(max(values.shape))
    spots = []
    for shift in (0, 1):
        where = [jax.random.randint(jax.random.fold_in(key, axis), (), 0, length) for axis, length in enumerate(values.shape)]
        where[longest] = (where[longest] + shift) % values.shape[longest]
        spots.append(tuple(where))
    return values.at[spots[0]].set(smallest).at[spots[1]].set(largest)


def block_scale(key, extent, split, smallest, top_value):
    def one(dim, blocks):
        draws = jax.random.uniform(jax.random.fold_in(jax.random.fold_in(key, 6), dim), (blocks,), jnp.float32, smallest / len(split), top_value / len(split))
        return jnp.repeat(jnp.exp(draws), extent[dim] // blocks).reshape((-1,) + (1,) * (len(extent) - dim - 1))

    level = one(*split[0])
    for cut in split[1:]:
        level = level * one(*cut)
    return level


def bell_draw(stream_key, extent, width, bound, shards=(), held_as=jnp.bfloat16):
    loudness = block_scale(stream_key, extent, shards, -0.22, 0.18) if shards else 1.0
    values = jax.random.normal(stream_key, extent, jnp.float32) * width * loudness
    return jnp.minimum(jnp.maximum(values, -bound), bound).astype(held_as)


def setup_inputs(seed: int = 0) -> dict:
    keys = jax.random.split(jax.random.key(seed), 7)
    pair_elems = bell_draw(keys[0], (PAIRS, 2, NPW), (3.0 / PAIRS ** 0.25), 3.171875, ((0, 1024),))
    slot_pair = jax.random.permutation(keys[1], PAIRS).astype(jnp.int32)
    val_index = plant(jax.random.randint(keys[2], (PAIRS,), 0, NVAL), jax.random.fold_in(keys[2], 1), 0, NVAL - 1).astype(jnp.int32)
    cond_index = plant(jax.random.randint(keys[3], (PAIRS,), 0, NCOND), jax.random.fold_in(keys[3], 1), 0, NCOND - 1).astype(jnp.int32)
    val_energy = jnp.clip(jax.random.uniform(keys[4], (NVAL,), jnp.float32, -12.0, -1.0), -12.0, -1.0)
    cond_energy = jnp.clip(jax.random.uniform(keys[5], (NCOND,), jnp.float32, 0.5, 10.0), 0.5, 10.0)
    return dict(pair_elems=pair_elems, slot_pair=slot_pair, val_index=val_index, cond_index=cond_index, val_energy=val_energy, cond_energy=cond_energy)


def reference(pair_elems, slot_pair, val_index, cond_index, val_energy, cond_energy):
    owner = slot_pair.astype(jnp.int32)
    upper = jnp.take(val_energy, jnp.take(val_index, owner))
    lower = jnp.take(cond_energy, jnp.take(cond_index, owner))
    weight = 2.0 / (upper - lower)
    scaled = (weight[:, None, None] * pair_elems.astype(jnp.float32)).astype(jnp.bfloat16)
    real_left = scaled.reshape(PAIRS * 2, NPW)
    imag_left = jnp.stack([scaled[:, 1], -scaled[:, 0]], axis=1).reshape(PAIRS * 2, NPW)
    right = pair_elems.reshape(PAIRS * 2, NPW)
    dims = (((0,), (0,)), ((), ()))
    real_part = lax.dot_general(real_left, right, dims, preferred_element_type=jnp.float32)
    imag_part = lax.dot_general(imag_left, right, dims, preferred_element_type=jnp.float32)
    return jnp.stack([real_part, imag_part])
```

```python
import jax
import jax.numpy as jnp
from jax import lax
from jax.experimental import pallas as pl
from jax.experimental.pallas import tpu as pltpu
from jax.sharding import PartitionSpec as P

LANES = 128
BF16 = jnp.bfloat16
F32 = jnp.float32
VMEM = pl.BlockSpec(memory_space=pltpu.VMEM)
SMEM = pl.BlockSpec(memory_space=pltpu.SMEM)
LIMIT = pltpu.CompilerParams(vmem_limit_bytes=48 * 1024 * 1024)


def split_right(elems, n_col):
    width = elems.shape[2] // n_col

    def kernel(in_ref, out_ref):
        for block in range(n_col):
            out_ref[block] = in_ref[0, :, block * width : (block + 1) * width]

    return pl.pallas_call(
        kernel,
        out_shape=jax.ShapeDtypeStruct((n_col, 2, width), BF16),
        in_specs=[VMEM],
        out_specs=VMEM,
        compiler_params=LIMIT,
    )(elems)


def split_left(elems, tables, position, n_row, span):
    full = elems.shape[2]
    width = full // n_row

    def kernel(where_ref, slot_ref, val_ref, cond_ref, upper_ref, lower_ref, in_ref, out_ref):
        owner = slot_ref[where_ref[0]]
        gap = upper_ref[val_ref[owner]] - lower_ref[cond_ref[owner]]
        weight = 2.0 / jnp.full((2, LANES), gap, F32)
        for tile in range(full // LANES):
            part = in_ref[0, :, tile * LANES : (tile + 1) * LANES]
            part = (weight * part.astype(F32)).astype(BF16)
            for block in range(n_row):
                place = tile - block * width // LANES
                if 0 <= place < span // LANES:
                    out_ref[block, :, place * LANES : (place + 1) * LANES] = part

    return pl.pallas_call(
        kernel,
        out_shape=jax.ShapeDtypeStruct((n_row, 2, span), BF16),
        in_specs=[SMEM] * 6 + [VMEM],
        out_specs=VMEM,
        compiler_params=LIMIT,
    )(position, *tables, elems)


def part_rows(slots):
    count, _, width = slots.shape

    def kernel(in_ref, out_ref):
        for tile in range(width // LANES):
            cut = slice(tile * LANES, (tile + 1) * LANES)
            both = in_ref[:, :, cut].astype(F32)
            out_ref[:count, cut] = both[:, 0, :].astype(BF16)
            out_ref[count:, cut] = both[:, 1, :].astype(BF16)

    return pl.pallas_call(
        kernel,
        out_shape=jax.ShapeDtypeStruct((2 * count, width), BF16),
        in_specs=[VMEM],
        out_specs=VMEM,
        compiler_params=LIMIT,
    )(slots)


def order_left(rows, shift, n_row, n_col, width):
    depth, span = rows.shape
    group = 2 * n_col

    def kernel(shift_ref, in_ref, out_ref, real_ref, imag_ref, turn_ref):
        off = pl.multiple_of(shift_ref[0], 64)
        for col in range(n_col):
            base = col * 2 * n_row
            first = pl.ds(col, n_row, stride=group)
            second = pl.ds(n_col + col, n_row, stride=group)
            for tile in range(span // LANES):
                cut = slice(tile * LANES, (tile + 1) * LANES)
                re = in_ref[base : base + n_row, cut].astype(F32)
                im = in_ref[base + n_row : base + 2 * n_row, cut].astype(F32)
                real_ref[tile, first, :] = re
                real_ref[tile, second, :] = im
                imag_ref[tile, first, :] = im
                imag_ref[tile, second, :] = -re
        step = min(256, depth)
        for which, source in enumerate((real_ref, imag_ref)):
            for tile in range(span // LANES):
                cut = slice(tile * LANES, (tile + 1) * LANES)
                for at in range(0, depth, step):
                    turn_ref[cut, at : at + step] = source[tile, at : at + step, :].T.astype(BF16)
            out_ref[which] = turn_ref[pl.ds(off, width), :]

    return pl.pallas_call(
        kernel,
        out_shape=jax.ShapeDtypeStruct((2, width, depth), BF16),
        in_specs=[SMEM, VMEM],
        out_specs=VMEM,
        scratch_shapes=[
            pltpu.VMEM((span // LANES, depth, LANES), F32),
            pltpu.VMEM((span // LANES, depth, LANES), F32),
            pltpu.VMEM((span, depth), BF16),
        ],
        compiler_params=LIMIT,
    )(shift, rows)


def multiply(left, right):
    _, width, depth = left.shape
    columns = right.shape[1]
    step = 256

    def kernel(left_ref, right_ref, out_ref):
        for which in range(2):
            out_ref[which] = jnp.dot(left_ref[which], right_ref[...], preferred_element_type=F32)

    return pl.pallas_call(
        kernel,
        grid=(columns // step,),
        out_shape=jax.ShapeDtypeStruct((2, width, columns), F32),
        in_specs=[
            pl.BlockSpec((2, width, depth), lambda j: (0, 0, 0)),
            pl.BlockSpec((depth, step), lambda j: (0, j)),
        ],
        out_specs=pl.BlockSpec((2, width, step), lambda j: (0, 0, j)),
        compiler_params=LIMIT,
        cost_estimate=pl.CostEstimate(
            flops=4 * width * depth * columns,
            bytes_accessed=2 * depth * (2 * width + columns) + 8 * width * columns,
            transcendentals=0,
        ),
    )(left, right)


def local(pair_elems, slot_pair, val_index, cond_index, val_energy, cond_energy):
    full = pair_elems.shape[2]
    n_row = lax.axis_size("row")
    n_col = lax.axis_size("col")
    row = lax.axis_index("row")
    position = (row * n_col + lax.axis_index("col")).astype(jnp.int32).reshape(1)
    width = full // n_row
    span = 3 * LANES

    right = split_right(pair_elems, n_col)
    right = lax.all_to_all(right, "col", split_axis=0, concat_axis=0, tiled=True)
    right = lax.all_gather(part_rows(right), "row", axis=0, tiled=True)

    tables = (slot_pair, val_index, cond_index, val_energy, cond_energy)
    left = split_left(pair_elems, tables, position, n_row, span)
    left = lax.all_to_all(left, "row", split_axis=0, concat_axis=0, tiled=True)
    left = part_rows(left)
    left = jnp.broadcast_to(left[None], (n_col, *left.shape))
    left = lax.all_to_all(left, "col", split_axis=0, concat_axis=0, tiled=True)
    left = left.reshape(n_col * left.shape[1], span)
    shift = (lax.rem(row * width, LANES)).astype(jnp.int32).reshape(1)
    left = order_left(left, shift, n_row, n_col, width)
    return multiply(left, right)


def solution(mesh):
    in_specs = (P(("row", "col"), None, None), P(), P(), P(), P(), P())
    out_specs = P(None, "row", "col")
    return jax.shard_map(local, mesh=mesh, in_specs=in_specs, out_specs=out_specs, check_vma=False)
```

```python
import jax
import jax.numpy as jnp
from jax import lax
from jax.experimental import pallas as pl
from jax.experimental.pallas import tpu as pltpu
from jax.sharding import Mesh
from jax.sharding import PartitionSpec as P

LANES = 128
ROW = ("z", "yh", "core")
COL = ("yl", "x")
BF16 = jnp.bfloat16
F32 = jnp.float32
VMEM = pl.BlockSpec(memory_space=pltpu.VMEM)
SMEM = pl.BlockSpec(memory_space=pltpu.SMEM)
LIMIT = pltpu.CompilerParams(vmem_limit_bytes=48 * 1024 * 1024)
WHOLE = pltpu.CompilerParams(vmem_limit_bytes=60 * 1024 * 1024)


def split_right(elems, n_col):
    width = elems.shape[2] // n_col

    def kernel(in_ref, out_ref):
        for block in range(n_col):
            out_ref[block] = in_ref[0, :, block * width : (block + 1) * width]

    return pl.pallas_call(
        kernel,
        out_shape=jax.ShapeDtypeStruct((n_col, 2, width), BF16),
        in_specs=[VMEM],
        out_specs=VMEM,
        compiler_params=WHOLE,
    )(elems)


def split_left(elems, tables, position, n_row, span, place_of):
    full = elems.shape[2]
    width = full // n_row

    def kernel(where_ref, slot_ref, val_ref, cond_ref, upper_ref, lower_ref, in_ref, out_ref):
        owner = slot_ref[where_ref[0]]
        gap = upper_ref[val_ref[owner]] - lower_ref[cond_ref[owner]]
        weight = 2.0 / jnp.full((2, LANES), gap, F32)
        for tile in range(full // LANES):
            part = in_ref[0, :, tile * LANES : (tile + 1) * LANES]
            part = (weight * part.astype(F32)).astype(BF16)
            for block in range(n_row):
                place = tile - block * width // LANES
                if 0 <= place < span // LANES:
                    slab = place_of(block)
                    out_ref[slab, :, place * LANES : (place + 1) * LANES] = part

    return pl.pallas_call(
        kernel,
        out_shape=jax.ShapeDtypeStruct((n_row, 2, span), BF16),
        in_specs=[SMEM] * 6 + [VMEM],
        out_specs=VMEM,
        compiler_params=WHOLE,
    )(position, *tables, elems)


def part_rows(slots):
    count, _, width = slots.shape

    def kernel(in_ref, out_ref):
        for tile in range(width // LANES):
            cut = slice(tile * LANES, (tile + 1) * LANES)
            both = in_ref[:, :, cut].astype(F32)
            out_ref[:count, cut] = both[:, 0, :].astype(BF16)
            out_ref[count:, cut] = both[:, 1, :].astype(BF16)

    return pl.pallas_call(
        kernel,
        out_shape=jax.ShapeDtypeStruct((2 * count, width), BF16),
        in_specs=[VMEM],
        out_specs=VMEM,
        compiler_params=LIMIT,
    )(slots)


def pack_left(slots, shift):
    count = slots.shape[0]
    half = LANES // 2

    def kernel(shift_ref, in_ref, out_ref):
        low = lax.broadcasted_iota(jnp.int32, (count, LANES), 1) < half
        moved = jnp.full((count, LANES), shift_ref[0], jnp.int32) > 0
        tiles = [in_ref[:, :, t * LANES : (t + 1) * LANES].astype(F32) for t in range(3)]
        ends = []
        for part in range(2):
            now = [tile[:, part, :] for tile in tiles]
            swapped = [pltpu.roll(tile, half, 1) for tile in now]
            for t in range(2):
                ahead = jnp.where(low, swapped[t], swapped[t + 1])
                slab = 2 * part + t
                out_ref[slab * count : (slab + 1) * count, :] = jnp.where(moved, ahead, now[t]).astype(BF16)
            ends.append(jnp.where(moved, swapped[2], now[2]))
        out_ref[4 * count :, :] = jnp.where(low, ends[0], pltpu.roll(ends[1], half, 1)).astype(BF16)

    return pl.pallas_call(
        kernel,
        out_shape=jax.ShapeDtypeStruct((5 * count, LANES), BF16),
        in_specs=[SMEM, VMEM],
        out_specs=VMEM,
        compiler_params=LIMIT,
    )(shift, slots)


def order_left(slabs, n_row, n_col, width):
    depth = 2 * n_row * n_col
    half = LANES // 2
    slots = 5 * n_row

    def kernel(in_ref, out_ref, real_ref, imag_ref):
        for col in range(n_col):
            first = pl.ds(col, n_row, stride=2 * n_col)
            second = pl.ds(n_col + col, n_row, stride=2 * n_col)
            rows = []
            for slab in range(5):
                at = col * slots + slab * n_row
                rows.append(in_ref[at : at + n_row, :].astype(F32))
            rows = [(rows[0], rows[2]), (rows[1], rows[3]), (rows[4], pltpu.roll(rows[4], half, 1))]
            for tile, (re, im) in enumerate(rows):
                real_ref[tile, first, :] = re
                real_ref[tile, second, :] = im
                imag_ref[tile, first, :] = im
                imag_ref[tile, second, :] = -re
        step = min(256, depth)
        for which, source in enumerate((real_ref, imag_ref)):
            for tile in range(3):
                keep = min(LANES, width - tile * LANES)
                for at in range(0, depth, step):
                    turned = source[tile, at : at + step, :].T.astype(BF16)
                    out_ref[which, tile * LANES : tile * LANES + keep, at : at + step] = turned[:keep]

    return pl.pallas_call(
        kernel,
        out_shape=jax.ShapeDtypeStruct((2, width, depth), BF16),
        in_specs=[VMEM],
        out_specs=VMEM,
        scratch_shapes=[pltpu.VMEM((3, depth, LANES), F32), pltpu.VMEM((3, depth, LANES), F32)],
        compiler_params=LIMIT,
    )(slabs)


def multiply(half, left, right, total=None):
    depth, columns = right.shape
    width = left.shape[1]
    step = 256

    def kernel(half_ref, left_ref, right_ref, *refs):
        out_ref = refs[-1]
        for which in range(2):
            product = jnp.dot(left_ref[which], right_ref[...], preferred_element_type=F32)
            out_ref[which] = product if total is None else refs[0][which] + product

    out_spec = pl.BlockSpec((2, width, step), lambda j, half_ref: (0, 0, j))
    extra = [] if total is None else [total]
    return pl.pallas_call(
        kernel,
        grid_spec=pltpu.PrefetchScalarGridSpec(
            num_scalar_prefetch=1,
            grid=(columns // step,),
            in_specs=[
                pl.BlockSpec((2, width, depth), lambda j, half_ref: (0, 0, half_ref[0])),
                pl.BlockSpec((depth, step), lambda j, half_ref: (0, j)),
            ]
            + [out_spec] * len(extra),
            out_specs=out_spec,
        ),
        out_shape=jax.ShapeDtypeStruct((2, width, columns), F32),
        input_output_aliases={3: 0} if extra else {},
        compiler_params=LIMIT,
        cost_estimate=pl.CostEstimate(
            flops=4 * width * depth * columns,
            bytes_accessed=2 * depth * (2 * width + columns) + 8 * width * columns,
            transcendentals=0,
        ),
    )(half, left, right, *extra)


def local(pair_elems, slot_pair, val_index, cond_index, val_energy, cond_energy):
    full = pair_elems.shape[2]
    n_row = lax.axis_size(ROW)
    n_col = lax.axis_size(COL)
    row = lax.axis_index(ROW)
    core = lax.axis_index("core").astype(jnp.int32).reshape(1)
    position = (row * n_col + lax.axis_index(COL)).astype(jnp.int32).reshape(1)
    width = full // n_row
    span = 3 * LANES

    def place_of(block):
        return block % 2 * (n_row // 2) + block // 2

    right = split_right(pair_elems, n_col)
    right = lax.all_to_all(right, COL, split_axis=0, concat_axis=0, tiled=True)

    tables = (slot_pair, val_index, cond_index, val_energy, cond_energy)
    left = split_left(pair_elems, tables, position, n_row, span, place_of)
    left = lax.all_to_all(left, ("core", "z", "yh"), split_axis=0, concat_axis=0, tiled=True)

    right = lax.all_gather(part_rows(right), ("z", "yh"), axis=0, tiled=True)
    shift = lax.rem(row * width, LANES).astype(jnp.int32).reshape(1)
    left = pack_left(left, shift)
    left = jnp.broadcast_to(left[None], (n_col, *left.shape))
    left = lax.all_to_all(left, COL, split_axis=0, concat_axis=0, tiled=True)
    left = order_left(left.reshape(n_col * left.shape[1], LANES), n_row, n_col, width)
    right, left = lax.optimization_barrier((right, left))

    other = lax.ppermute(right, "core", [(0, 1), (1, 0)])
    total = multiply(core, left, right)
    return multiply(1 - core, left, other, total)


def solution(mesh):
    n_row, n_col = mesh.devices.shape
    torus = Mesh(mesh.devices.reshape(n_row // 8, 4, 2, 2, n_col // 2), (*ROW, *COL))
    in_specs = (P((*ROW, *COL), None, None), P(), P(), P(), P(), P())
    out_specs = P(None, ROW, COL)
    return jax.shard_map(local, mesh=torus, in_specs=in_specs, out_specs=out_specs, check_vma=False)
```

```python
import jax
import jax.numpy as jnp
from jax import lax
from jax.experimental import pallas as pl
from jax.experimental.pallas import tpu as pltpu
from jax.sharding import Mesh
from jax.sharding import PartitionSpec as P

LANES = 128
ROW = ("z", "yh", "core")
COL = ("yl", "x")
BF16 = jnp.bfloat16
F32 = jnp.float32
VMEM = pl.BlockSpec(memory_space=pltpu.VMEM)
SMEM = pl.BlockSpec(memory_space=pltpu.SMEM)
LIMIT = pltpu.CompilerParams(vmem_limit_bytes=48 * 1024 * 1024)
WHOLE = pltpu.CompilerParams(vmem_limit_bytes=60 * 1024 * 1024)


def split_right(elems, n_col, copies):
    width = elems.shape[2] // n_col

    def kernel(in_ref, out_ref):
        for block in range(n_col):
            part = in_ref[0, :, block * width : (block + 1) * width]
            for copy in range(copies):
                out_ref[copy * n_col + block] = part

    return pl.pallas_call(
        kernel,
        out_shape=jax.ShapeDtypeStruct((copies * n_col, 2, width), BF16),
        in_specs=[VMEM],
        out_specs=VMEM,
        compiler_params=WHOLE,
    )(elems)


def split_left(elems, tables, position, n_row, span, place_of):
    full = elems.shape[2]
    width = full // n_row

    def kernel(where_ref, slot_ref, val_ref, cond_ref, upper_ref, lower_ref, in_ref, out_ref):
        owner = slot_ref[where_ref[0]]
        gap = upper_ref[val_ref[owner]] - lower_ref[cond_ref[owner]]
        weight = 2.0 / jnp.full((2, LANES), gap, F32)
        for tile in range(full // LANES):
            part = in_ref[0, :, tile * LANES : (tile + 1) * LANES]
            part = (weight * part.astype(F32)).astype(BF16)
            for block in range(n_row):
                place = tile - block * width // LANES
                if 0 <= place < span // LANES:
                    slab = place_of(block)
                    out_ref[slab, :, place * LANES : (place + 1) * LANES] = part

    return pl.pallas_call(
        kernel,
        out_shape=jax.ShapeDtypeStruct((n_row, 2, span), BF16),
        in_specs=[SMEM] * 6 + [VMEM],
        out_specs=VMEM,
        compiler_params=WHOLE,
    )(position, *tables, elems)


def part_rows(slots):
    count, _, width = slots.shape

    def kernel(in_ref, out_ref):
        for tile in range(width // LANES):
            cut = slice(tile * LANES, (tile + 1) * LANES)
            both = in_ref[:, :, cut].astype(F32)
            out_ref[:count, cut] = both[:, 0, :].astype(BF16)
            out_ref[count:, cut] = both[:, 1, :].astype(BF16)

    return pl.pallas_call(
        kernel,
        out_shape=jax.ShapeDtypeStruct((2 * count, width), BF16),
        in_specs=[VMEM],
        out_specs=VMEM,
        compiler_params=LIMIT,
    )(slots)


def pack_left(slots, shift):
    count = slots.shape[0]
    half = LANES // 2

    def kernel(shift_ref, in_ref, out_ref):
        low = lax.broadcasted_iota(jnp.int32, (count, LANES), 1) < half
        moved = jnp.full((count, LANES), shift_ref[0], jnp.int32) > 0
        tiles = [in_ref[:, :, t * LANES : (t + 1) * LANES].astype(F32) for t in range(3)]
        ends = []
        for part in range(2):
            now = [tile[:, part, :] for tile in tiles]
            swapped = [pltpu.roll(tile, half, 1) for tile in now]
            for t in range(2):
                ahead = jnp.where(low, swapped[t], swapped[t + 1])
                slab = 2 * part + t
                out_ref[slab * count : (slab + 1) * count, :] = jnp.where(moved, ahead, now[t]).astype(BF16)
            ends.append(jnp.where(moved, swapped[2], now[2]))
        out_ref[4 * count :, :] = jnp.where(low, ends[0], pltpu.roll(ends[1], half, 1)).astype(BF16)

    return pl.pallas_call(
        kernel,
        out_shape=jax.ShapeDtypeStruct((5 * count, LANES), BF16),
        in_specs=[SMEM, VMEM],
        out_specs=VMEM,
        compiler_params=LIMIT,
    )(shift, slots)


def order_left(slabs, n_row, n_col, n_far, width):
    group = n_row // n_far
    near = n_far * n_col
    depth = 2 * n_row * n_col
    half = LANES // 2
    slots = 5 * n_row

    def kernel(in_ref, out_ref, real_ref, imag_ref):
        for col in range(n_col):
            for far in range(n_far):
                first = pl.ds(far * n_col + col, group, stride=2 * near)
                second = pl.ds(near + far * n_col + col, group, stride=2 * near)
                rows = []
                for slab in range(5):
                    at = col * slots + slab * n_row + far * group
                    rows.append(in_ref[at : at + group, :].astype(F32))
                rows = [(rows[0], rows[2]), (rows[1], rows[3]), (rows[4], pltpu.roll(rows[4], half, 1))]
                for tile, (re, im) in enumerate(rows):
                    real_ref[tile, first, :] = re
                    real_ref[tile, second, :] = im
                    imag_ref[tile, first, :] = im
                    imag_ref[tile, second, :] = -re
        step = min(256, depth)
        for which, source in enumerate((real_ref, imag_ref)):
            for tile in range(3):
                keep = min(LANES, width - tile * LANES)
                for at in range(0, depth, step):
                    turned = source[tile, at : at + step, :].T.astype(BF16)
                    out_ref[which, tile * LANES : tile * LANES + keep, at : at + step] = turned[:keep]

    return pl.pallas_call(
        kernel,
        out_shape=jax.ShapeDtypeStruct((2, width, depth), BF16),
        in_specs=[VMEM],
        out_specs=VMEM,
        scratch_shapes=[pltpu.VMEM((3, depth, LANES), F32), pltpu.VMEM((3, depth, LANES), F32)],
        compiler_params=LIMIT,
    )(slabs)


def multiply(half, left, right, total=None):
    depth, columns = right.shape
    width = left.shape[1]
    step = 256

    def kernel(half_ref, left_ref, right_ref, *refs):
        out_ref = refs[-1]
        for which in range(2):
            product = jnp.dot(left_ref[which], right_ref[...], preferred_element_type=F32)
            out_ref[which] = product if total is None else refs[0][which] + product

    out_spec = pl.BlockSpec((2, width, step), lambda j, half_ref: (0, 0, j))
    extra = [] if total is None else [total]
    return pl.pallas_call(
        kernel,
        grid_spec=pltpu.PrefetchScalarGridSpec(
            num_scalar_prefetch=1,
            grid=(columns // step,),
            in_specs=[
                pl.BlockSpec((2, width, depth), lambda j, half_ref: (0, 0, half_ref[0])),
                pl.BlockSpec((depth, step), lambda j, half_ref: (0, j)),
            ]
            + [out_spec] * len(extra),
            out_specs=out_spec,
        ),
        out_shape=jax.ShapeDtypeStruct((2, width, columns), F32),
        input_output_aliases={3: 0} if extra else {},
        compiler_params=LIMIT,
        cost_estimate=pl.CostEstimate(
            flops=4 * width * depth * columns,
            bytes_accessed=2 * depth * (2 * width + columns) + 8 * width * columns,
            transcendentals=0,
        ),
    )(half, left, right, *extra)


def local(pair_elems, slot_pair, val_index, cond_index, val_energy, cond_energy):
    full = pair_elems.shape[2]
    n_row = lax.axis_size(ROW)
    n_col = lax.axis_size(COL)
    n_far = lax.axis_size("yh")
    n_z = lax.axis_size("z")
    row = lax.axis_index(ROW)
    core = lax.axis_index("core").astype(jnp.int32).reshape(1)
    position = (row * n_col + lax.axis_index(COL)).astype(jnp.int32).reshape(1)
    width = full // n_row
    span = 3 * LANES

    def place_of(block):
        z, far, side = block // (2 * n_far), block // 2 % n_far, block % 2
        return (far * 2 + side) * n_z + z

    tables = (slot_pair, val_index, cond_index, val_energy, cond_energy)
    left = split_left(pair_elems, tables, position, n_row, span, place_of)
    left = lax.all_to_all(left, ("yh", "core", "z"), split_axis=0, concat_axis=0, tiled=True)
    right = split_right(pair_elems, n_col, n_far)
    left, right = lax.optimization_barrier((left, right))
    right = lax.all_to_all(right, ("yh", *COL), split_axis=0, concat_axis=0, tiled=True)

    shift = lax.rem(row * width, LANES).astype(jnp.int32).reshape(1)
    left = pack_left(left, shift)
    left = jnp.broadcast_to(left[None], (n_col, *left.shape))
    right, left = lax.optimization_barrier((right, left))
    left = lax.all_to_all(left, COL, split_axis=0, concat_axis=0, tiled=True)
    right = lax.all_gather(part_rows(right), "z", axis=0, tiled=True)
    right, left = lax.optimization_barrier((right, left))

    other = lax.ppermute(right, "core", [(0, 1), (1, 0)])
    left = order_left(left.reshape(n_col * left.shape[1], LANES), n_row, n_col, n_far, width)
    total = multiply(core, left, right)
    return multiply(1 - core, left, other, total)


def solution(mesh):
    n_row, n_col = mesh.devices.shape
    torus = Mesh(mesh.devices.reshape(n_row // 8, 4, 2, 2, n_col // 2), (*ROW, *COL))
    in_specs = (P((*ROW, *COL), None, None), P(), P(), P(), P(), P())
    out_specs = P(None, ROW, COL)
    return jax.shard_map(local, mesh=torus, in_specs=in_specs, out_specs=out_specs, check_vma=False)
```

```python
import jax
import jax.numpy as jnp
from jax import lax
from jax.experimental import pallas as pl
from jax.experimental.pallas import tpu as pltpu
from jax.sharding import Mesh
from jax.sharding import PartitionSpec as P

LANES = 128
ROW = ("z", "yh", "core")
COL = ("yl", "x")
BF16 = jnp.bfloat16
F32 = jnp.float32
VMEM = pl.BlockSpec(memory_space=pltpu.VMEM)
SMEM = pl.BlockSpec(memory_space=pltpu.SMEM)
LIMIT = pltpu.CompilerParams(vmem_limit_bytes=48 * 1024 * 1024)
WHOLE = pltpu.CompilerParams(vmem_limit_bytes=60 * 1024 * 1024)


def split_right(elems, n_col, copies):
    width = elems.shape[2] // n_col

    def kernel(in_ref, out_ref):
        for block in range(n_col):
            part = in_ref[0, :, block * width : (block + 1) * width]
            for copy in range(copies):
                out_ref[copy * n_col + block] = part

    return pl.pallas_call(
        kernel,
        out_shape=jax.ShapeDtypeStruct((copies * n_col, 2, width), BF16),
        in_specs=[VMEM],
        out_specs=VMEM,
        compiler_params=WHOLE,
    )(elems)


def split_left(elems, tables, position, n_row, span, place_of):
    full = elems.shape[2]
    width = full // n_row

    def kernel(where_ref, slot_ref, val_ref, cond_ref, upper_ref, lower_ref, in_ref, out_ref):
        owner = slot_ref[where_ref[0]]
        gap = upper_ref[val_ref[owner]] - lower_ref[cond_ref[owner]]
        weight = 2.0 / jnp.full((2, LANES), gap, F32)
        for tile in range(full // LANES):
            part = in_ref[0, :, tile * LANES : (tile + 1) * LANES]
            part = (weight * part.astype(F32)).astype(BF16)
            for block in range(n_row):
                place = tile - block * width // LANES
                if 0 <= place < span // LANES:
                    slab = place_of(block)
                    out_ref[slab, :, place * LANES : (place + 1) * LANES] = part

    return pl.pallas_call(
        kernel,
        out_shape=jax.ShapeDtypeStruct((n_row, 2, span), BF16),
        in_specs=[SMEM] * 6 + [VMEM],
        out_specs=VMEM,
        compiler_params=WHOLE,
    )(position, *tables, elems)


def part_rows(slots):
    count, _, width = slots.shape

    def kernel(in_ref, out_ref):
        for tile in range(width // LANES):
            cut = slice(tile * LANES, (tile + 1) * LANES)
            both = in_ref[:, :, cut].astype(F32)
            out_ref[:count, cut] = both[:, 0, :].astype(BF16)
            out_ref[count:, cut] = both[:, 1, :].astype(BF16)

    return pl.pallas_call(
        kernel,
        out_shape=jax.ShapeDtypeStruct((2 * count, width), BF16),
        in_specs=[VMEM],
        out_specs=VMEM,
        compiler_params=LIMIT,
    )(slots)


def pack_left(slots, shift):
    count = slots.shape[0]
    half = LANES // 2

    def kernel(shift_ref, in_ref, out_ref):
        low = lax.broadcasted_iota(jnp.int32, (count, LANES), 1) < half
        moved = jnp.full((count, LANES), shift_ref[0], jnp.int32) > 0
        tiles = [in_ref[:, :, t * LANES : (t + 1) * LANES].astype(F32) for t in range(3)]
        ends = []
        for part in range(2):
            now = [tile[:, part, :] for tile in tiles]
            swapped = [pltpu.roll(tile, half, 1) for tile in now]
            for t in range(2):
                ahead = jnp.where(low, swapped[t], swapped[t + 1])
                slab = 2 * part + t
                out_ref[slab * count : (slab + 1) * count, :] = jnp.where(moved, ahead, now[t]).astype(BF16)
            ends.append(jnp.where(moved, swapped[2], now[2]))
        out_ref[4 * count :, :] = jnp.where(low, ends[0], pltpu.roll(ends[1], half, 1)).astype(BF16)

    return pl.pallas_call(
        kernel,
        out_shape=jax.ShapeDtypeStruct((5 * count, LANES), BF16),
        in_specs=[SMEM, VMEM],
        out_specs=VMEM,
        compiler_params=LIMIT,
    )(shift, slots)


def order_left(slabs, n_row, n_col, n_far, width):
    group = n_row // n_far
    near = n_far * n_col
    depth = 2 * n_row * n_col
    half = LANES // 2
    slots = 5 * n_row
    step = 2 * near

    def kernel(in_ref, out_ref, rows_ref):
        for col in range(n_col):
            for far in range(n_far):
                first = pl.ds(far * n_col + col, group, stride=step)
                second = pl.ds(near + far * n_col + col, group, stride=step)
                rows = []
                for slab in range(5):
                    at = col * slots + slab * n_row + far * group
                    rows.append(in_ref[at : at + group, :].astype(F32))
                rows = [(rows[0], rows[2]), (rows[1], rows[3]), (rows[4], pltpu.roll(rows[4], half, 1))]
                for tile, (re, im) in enumerate(rows):
                    rows_ref[tile, first, :] = re
                    rows_ref[tile, second, :] = im
        sign = jnp.where(lax.broadcasted_iota(jnp.int32, (LANES, step), 1) < near, 1.0, -1.0)
        for tile in range(3):
            keep = min(LANES, width - tile * LANES)
            here = slice(tile * LANES, tile * LANES + keep)
            for at in range(0, depth, step):
                turned = rows_ref[tile, at : at + step, :].T
                out_ref[0, here, at : at + step] = turned[:keep].astype(BF16)
                turned = pltpu.roll(turned, near, 1) * sign
                out_ref[1, here, at : at + step] = turned[:keep].astype(BF16)

    return pl.pallas_call(
        kernel,
        out_shape=jax.ShapeDtypeStruct((2, width, depth), BF16),
        in_specs=[VMEM],
        out_specs=VMEM,
        scratch_shapes=[pltpu.VMEM((3, depth, LANES), F32)],
        compiler_params=LIMIT,
    )(slabs)


def multiply(half, left, right, total=None):
    depth, columns = right.shape
    width = left.shape[1]
    step = 256

    def kernel(half_ref, left_ref, right_ref, *refs):
        out_ref = refs[-1]
        now = pl.ds(pl.multiple_of(pl.program_id(0) * step, step), step)
        for which in range(2):
            product = jnp.dot(left_ref[which], right_ref[:, now], preferred_element_type=F32)
            out_ref[which] = product if total is None else refs[0][which, :, now] + product

    extra = [] if total is None else [total]
    return pl.pallas_call(
        kernel,
        grid_spec=pltpu.PrefetchScalarGridSpec(
            num_scalar_prefetch=1,
            grid=(columns // step,),
            in_specs=[pl.BlockSpec((2, width, depth), lambda j, half_ref: (0, 0, half_ref[0])), VMEM]
            + [VMEM] * len(extra),
            out_specs=pl.BlockSpec((2, width, step), lambda j, half_ref: (0, 0, j)),
        ),
        out_shape=jax.ShapeDtypeStruct((2, width, columns), F32),
        compiler_params=LIMIT,
        cost_estimate=pl.CostEstimate(
            flops=4 * width * depth * columns,
            bytes_accessed=2 * depth * (2 * width + columns) + 8 * width * columns,
            transcendentals=0,
        ),
    )(half, left, right, *extra)


def local(pair_elems, slot_pair, val_index, cond_index, val_energy, cond_energy):
    full = pair_elems.shape[2]
    n_row = lax.axis_size(ROW)
    n_col = lax.axis_size(COL)
    n_far = lax.axis_size("yh")
    n_z = lax.axis_size("z")
    row = lax.axis_index(ROW)
    core = lax.axis_index("core").astype(jnp.int32).reshape(1)
    position = (row * n_col + lax.axis_index(COL)).astype(jnp.int32).reshape(1)
    width = full // n_row
    span = 3 * LANES

    def place_of(block):
        z, far, side = block // (2 * n_far), block // 2 % n_far, block % 2
        return (far * 2 + side) * n_z + z

    tables = (slot_pair, val_index, cond_index, val_energy, cond_energy)
    left = split_left(pair_elems, tables, position, n_row, span, place_of)
    left = lax.all_to_all(left, ("yh", "core", "z"), split_axis=0, concat_axis=0, tiled=True)
    right = split_right(pair_elems, n_col, n_far)
    left, right = lax.optimization_barrier((left, right))
    right = lax.all_to_all(right, ("yh", *COL), split_axis=0, concat_axis=0, tiled=True)

    shift = lax.rem(row * width, LANES).astype(jnp.int32).reshape(1)
    left = pack_left(left, shift)
    left = jnp.broadcast_to(left[None], (n_col, *left.shape))
    right, left = lax.optimization_barrier((right, left))
    left = lax.all_to_all(left, COL, split_axis=0, concat_axis=0, tiled=True)
    right = lax.all_gather(part_rows(right), "z", axis=0, tiled=True)
    left = order_left(left.reshape(n_col * left.shape[1], LANES), n_row, n_col, n_far, width)
    right, left = lax.optimization_barrier((right, left))

    other = lax.ppermute(right, "core", [(0, 1), (1, 0)])
    total = multiply(core, left, right)
    return multiply(1 - core, left, other, total)


def solution(mesh):
    n_row, n_col = mesh.devices.shape
    torus = Mesh(mesh.devices.reshape(n_row // 8, 4, 2, 2, n_col // 2), (*ROW, *COL))
    in_specs = (P((*ROW, *COL), None, None), P(), P(), P(), P(), P())
    out_specs = P(None, ROW, COL)
    return jax.shard_map(local, mesh=torus, in_specs=in_specs, out_specs=out_specs, check_vma=False)
```

```python
import jax
import jax.numpy as jnp
from jax import lax
from jax.experimental import pallas as pl
from jax.experimental.pallas import tpu as pltpu
from jax.sharding import Mesh
from jax.sharding import PartitionSpec as P

LANES = 128
ROW = ("z", "yh", "core")
COL = ("yl", "x")
BF16 = jnp.bfloat16
F32 = jnp.float32
VMEM = pl.BlockSpec(memory_space=pltpu.VMEM)
SMEM = pl.BlockSpec(memory_space=pltpu.SMEM)
LIMIT = pltpu.CompilerParams(vmem_limit_bytes=48 * 1024 * 1024)
SMALL = pltpu.CompilerParams(vmem_limit_bytes=32 * 1024 * 1024)
WHOLE = pltpu.CompilerParams(vmem_limit_bytes=60 * 1024 * 1024)


def split_right(elems, n_col, copies):
    width = elems.shape[2] // n_col

    def kernel(in_ref, out_ref):
        for block in range(n_col):
            part = in_ref[0, :, block * width : (block + 1) * width]
            for copy in range(copies):
                out_ref[copy * n_col + block] = part

    return pl.pallas_call(
        kernel,
        out_shape=jax.ShapeDtypeStruct((copies * n_col, 2, width), BF16),
        in_specs=[VMEM],
        out_specs=VMEM,
        compiler_params=WHOLE,
    )(elems)


def split_left(elems, tables, position, n_row, span, place_of):
    full = elems.shape[2]
    width = full // n_row

    def kernel(where_ref, slot_ref, val_ref, cond_ref, upper_ref, lower_ref, in_ref, out_ref):
        owner = slot_ref[where_ref[0]]
        gap = upper_ref[val_ref[owner]] - lower_ref[cond_ref[owner]]
        weight = 2.0 / jnp.full((2, LANES), gap, F32)
        for tile in range(full // LANES):
            part = in_ref[0, :, tile * LANES : (tile + 1) * LANES]
            part = (weight * part.astype(F32)).astype(BF16)
            for block in range(n_row):
                place = tile - block * width // LANES
                if 0 <= place < span // LANES:
                    slab = place_of(block)
                    out_ref[slab, :, place * LANES : (place + 1) * LANES] = part

    return pl.pallas_call(
        kernel,
        out_shape=jax.ShapeDtypeStruct((n_row, 2, span), BF16),
        in_specs=[SMEM] * 6 + [VMEM],
        out_specs=VMEM,
        compiler_params=WHOLE,
    )(position, *tables, elems)


def part_rows(slots):
    count, _, width = slots.shape

    def kernel(in_ref, out_ref):
        for tile in range(width // LANES):
            cut = slice(tile * LANES, (tile + 1) * LANES)
            both = in_ref[:, :, cut].astype(F32)
            out_ref[:count, cut] = both[:, 0, :].astype(BF16)
            out_ref[count:, cut] = both[:, 1, :].astype(BF16)

    return pl.pallas_call(
        kernel,
        out_shape=jax.ShapeDtypeStruct((2 * count, width), BF16),
        in_specs=[VMEM],
        out_specs=VMEM,
        compiler_params=LIMIT,
    )(slots)


def pack_left(slots, shift):
    count = slots.shape[0]
    half = LANES // 2

    def kernel(shift_ref, in_ref, out_ref):
        low = lax.broadcasted_iota(jnp.int32, (count, LANES), 1) < half
        moved = jnp.full((count, LANES), shift_ref[0], jnp.int32) > 0
        tiles = [in_ref[:, :, t * LANES : (t + 1) * LANES].astype(F32) for t in range(3)]
        ends = []
        for part in range(2):
            now = [tile[:, part, :] for tile in tiles]
            swapped = [pltpu.roll(tile, half, 1) for tile in now]
            for t in range(2):
                ahead = jnp.where(low, swapped[t], swapped[t + 1])
                slab = 2 * part + t
                out_ref[slab * count : (slab + 1) * count, :] = jnp.where(moved, ahead, now[t]).astype(BF16)
            ends.append(jnp.where(moved, swapped[2], now[2]))
        out_ref[4 * count :, :] = jnp.where(low, ends[0], pltpu.roll(ends[1], half, 1)).astype(BF16)

    return pl.pallas_call(
        kernel,
        out_shape=jax.ShapeDtypeStruct((5 * count, LANES), BF16),
        in_specs=[SMEM, VMEM],
        out_specs=VMEM,
        compiler_params=LIMIT,
    )(shift, slots)


def order_left(slabs, n_row, n_col, n_far, width):
    group = n_row // n_far
    near = n_far * n_col
    depth = 2 * n_row * n_col
    half = LANES // 2
    slots = 5 * n_row
    step = 2 * near

    def kernel(in_ref, out_ref, rows_ref):
        for col in range(n_col):
            for far in range(n_far):
                first = pl.ds(far * n_col + col, group, stride=step)
                second = pl.ds(near + far * n_col + col, group, stride=step)
                rows = []
                for slab in range(5):
                    at = col * slots + slab * n_row + far * group
                    rows.append(in_ref[at : at + group, :].astype(F32))
                rows = [(rows[0], rows[2]), (rows[1], rows[3]), (rows[4], pltpu.roll(rows[4], half, 1))]
                for tile, (re, im) in enumerate(rows):
                    rows_ref[tile, first, :] = re
                    rows_ref[tile, second, :] = im
        sign = jnp.where(lax.broadcasted_iota(jnp.int32, (LANES, step), 1) < near, 1.0, -1.0)
        for tile in range(3):
            keep = min(LANES, width - tile * LANES)
            here = slice(tile * LANES, tile * LANES + keep)
            for at in range(0, depth, step):
                turned = rows_ref[tile, at : at + step, :].T
                out_ref[0, here, at : at + step] = turned[:keep].astype(BF16)
                turned = pltpu.roll(turned, near, 1) * sign
                out_ref[1, here, at : at + step] = turned[:keep].astype(BF16)

    return pl.pallas_call(
        kernel,
        out_shape=jax.ShapeDtypeStruct((2, width, depth), BF16),
        in_specs=[VMEM],
        out_specs=VMEM,
        scratch_shapes=[pltpu.VMEM((3, depth, LANES), F32)],
        compiler_params=LIMIT,
    )(slabs)


def multiply(half, left, right, total=None):
    depth, columns = right.shape
    width = left.shape[1]
    step = 256

    def kernel(half_ref, left_ref, right_ref, *refs):
        now = pl.ds(pl.multiple_of(pl.program_id(0) * step, step), step)
        for which in range(2):
            product = jnp.dot(left_ref[which], right_ref[:, now] if extra else right_ref[...], preferred_element_type=F32)
            if total is None:
                refs[0][which, :, now] = product
            else:
                refs[1][which] = refs[0][which, :, now] + product

    extra = [] if total is None else [total]
    return pl.pallas_call(
        kernel,
        grid_spec=pltpu.PrefetchScalarGridSpec(
            num_scalar_prefetch=1,
            grid=(columns // step,),
            in_specs=[pl.BlockSpec((2, width, depth), lambda j, half_ref: (0, 0, half_ref[0])), VMEM if extra else pl.BlockSpec((depth, step), lambda j, half_ref: (0, j))]
            + [VMEM] * len(extra),
            out_specs=pl.BlockSpec((2, width, step), lambda j, half_ref: (0, 0, j)) if extra else VMEM,
        ),
        out_shape=jax.ShapeDtypeStruct((2, width, columns), F32),
        compiler_params=SMALL,
        cost_estimate=pl.CostEstimate(
            flops=4 * width * depth * columns,
            bytes_accessed=2 * depth * (2 * width + columns) + 8 * width * columns,
            transcendentals=0,
        ),
    )(half, left, right, *extra)


def local(pair_elems, slot_pair, val_index, cond_index, val_energy, cond_energy):
    full = pair_elems.shape[2]
    n_row = lax.axis_size(ROW)
    n_col = lax.axis_size(COL)
    n_far = lax.axis_size("yh")
    n_z = lax.axis_size("z")
    row = lax.axis_index(ROW)
    core = lax.axis_index("core").astype(jnp.int32).reshape(1)
    position = (row * n_col + lax.axis_index(COL)).astype(jnp.int32).reshape(1)
    width = full // n_row
    span = 3 * LANES

    def place_of(block):
        z, far, side = block // (2 * n_far), block // 2 % n_far, block % 2
        return (far * 2 + side) * n_z + z

    tables = (slot_pair, val_index, cond_index, val_energy, cond_energy)
    left = split_left(pair_elems, tables, position, n_row, span, place_of)
    left = lax.all_to_all(left, ("yh", "core", "z"), split_axis=0, concat_axis=0, tiled=True)
    right = split_right(pair_elems, n_col, n_far)
    left, right = lax.optimization_barrier((left, right))
    right = lax.all_to_all(right, ("yh", *COL), split_axis=0, concat_axis=0, tiled=True)

    shift = lax.rem(row * width, LANES).astype(jnp.int32).reshape(1)
    left = pack_left(left, shift)
    left = jnp.broadcast_to(left[None], (n_col, *left.shape))
    right, left = lax.optimization_barrier((right, left))
    left = lax.all_to_all(left, COL, split_axis=0, concat_axis=0, tiled=True)
    right = lax.all_gather(part_rows(right), "z", axis=0, tiled=True)
    left = order_left(left.reshape(n_col * left.shape[1], LANES), n_row, n_col, n_far, width)
    right, left = lax.optimization_barrier((right, left))

    other = lax.ppermute(right, "core", [(0, 1), (1, 0)])
    total = multiply(core, left, right)
    return multiply(1 - core, left, other, total)


def solution(mesh):
    n_row, n_col = mesh.devices.shape
    torus = Mesh(mesh.devices.reshape(n_row // 8, 4, 2, 2, n_col // 2), (*ROW, *COL))
    in_specs = (P((*ROW, *COL), None, None), P(), P(), P(), P(), P())
    out_specs = P(None, ROW, COL)
    return jax.shard_map(local, mesh=torus, in_specs=in_specs, out_specs=out_specs, check_vma=False)
```

```python
import jax
import jax.numpy as jnp
from jax import lax
from jax.experimental import pallas as pl
from jax.experimental.pallas import tpu as pltpu
from jax.sharding import Mesh
from jax.sharding import PartitionSpec as P

LANES = 128
ROW = ("z", "yh", "core")
COL = ("yl", "x")
BF16 = jnp.bfloat16
F32 = jnp.float32
VMEM = pl.BlockSpec(memory_space=pltpu.VMEM)
SMEM = pl.BlockSpec(memory_space=pltpu.SMEM)
LIMIT = pltpu.CompilerParams(vmem_limit_bytes=48 * 1024 * 1024)
SMALL = pltpu.CompilerParams(vmem_limit_bytes=32 * 1024 * 1024)
WHOLE = pltpu.CompilerParams(vmem_limit_bytes=60 * 1024 * 1024)


def split_right(elems, n_col):
    width = elems.shape[2] // n_col

    def kernel(in_ref, out_ref):
        for block in range(n_col):
            out_ref[block] = in_ref[0, :, block * width : (block + 1) * width]

    return pl.pallas_call(
        kernel,
        out_shape=jax.ShapeDtypeStruct((n_col, 2, width), BF16),
        in_specs=[VMEM],
        out_specs=VMEM,
        compiler_params=WHOLE,
    )(elems)


def split_left(elems, tables, position, n_row, span, place_of):
    full = elems.shape[2]
    width = full // n_row

    def kernel(where_ref, slot_ref, val_ref, cond_ref, upper_ref, lower_ref, in_ref, out_ref):
        owner = slot_ref[where_ref[0]]
        gap = upper_ref[val_ref[owner]] - lower_ref[cond_ref[owner]]
        weight = 2.0 / jnp.full((2, LANES), gap, F32)
        for tile in range(full // LANES):
            part = in_ref[0, :, tile * LANES : (tile + 1) * LANES]
            part = (weight * part.astype(F32)).astype(BF16)
            for block in range(n_row):
                place = tile - block * width // LANES
                if 0 <= place < span // LANES:
                    slab = place_of(block)
                    out_ref[slab, :, place * LANES : (place + 1) * LANES] = part

    return pl.pallas_call(
        kernel,
        out_shape=jax.ShapeDtypeStruct((n_row, 2, span), BF16),
        in_specs=[SMEM] * 6 + [VMEM],
        out_specs=VMEM,
        compiler_params=WHOLE,
    )(position, *tables, elems)


def part_rows(groups):
    count, _, width = groups[0].shape
    total = len(groups) * count

    def kernel(*refs):
        out_ref = refs[-1]
        for tile in range(width // LANES):
            cut = slice(tile * LANES, (tile + 1) * LANES)
            for place, in_ref in enumerate(refs[:-1]):
                both = in_ref[:, :, cut].astype(F32)
                at = place * count
                out_ref[at : at + count, cut] = both[:, 0, :].astype(BF16)
                out_ref[total + at : total + at + count, cut] = both[:, 1, :].astype(BF16)

    return pl.pallas_call(
        kernel,
        out_shape=jax.ShapeDtypeStruct((2 * total, width), BF16),
        in_specs=[VMEM] * len(groups),
        out_specs=VMEM,
        compiler_params=LIMIT,
    )(*groups)


def pack_left(slots, shift):
    count = slots.shape[0]
    half = LANES // 2

    def kernel(shift_ref, in_ref, out_ref):
        low = lax.broadcasted_iota(jnp.int32, (count, LANES), 1) < half
        moved = jnp.full((count, LANES), shift_ref[0], jnp.int32) > 0
        tiles = [in_ref[:, :, t * LANES : (t + 1) * LANES].astype(F32) for t in range(3)]
        ends = []
        for part in range(2):
            now = [tile[:, part, :] for tile in tiles]
            swapped = [pltpu.roll(tile, half, 1) for tile in now]
            for t in range(2):
                ahead = jnp.where(low, swapped[t], swapped[t + 1])
                slab = 2 * part + t
                out_ref[slab * count : (slab + 1) * count, :] = jnp.where(moved, ahead, now[t]).astype(BF16)
            ends.append(jnp.where(moved, swapped[2], now[2]))
        out_ref[4 * count :, :] = jnp.where(low, ends[0], pltpu.roll(ends[1], half, 1)).astype(BF16)

    return pl.pallas_call(
        kernel,
        out_shape=jax.ShapeDtypeStruct((5 * count, LANES), BF16),
        in_specs=[SMEM, VMEM],
        out_specs=VMEM,
        compiler_params=LIMIT,
    )(shift, slots)


def order_left(here, slabs, n_row, n_col, n_far, width):
    group = n_row // n_far
    near = n_far * n_col
    depth = 2 * n_row * n_col
    half = LANES // 2
    slots = 5 * n_row
    step = 2 * near

    def kernel(here_ref, in_ref, out_ref, rows_ref):
        for col in range(n_col):
            for far in range(n_far):
                held = lax.rem(here_ref[0] + far, n_far)
                first = pl.ds(far * n_col + col, group, stride=step)
                second = pl.ds(near + far * n_col + col, group, stride=step)
                rows = []
                for slab in range(5):
                    at = pl.multiple_of(col * slots + slab * n_row + held * group, group)
                    rows.append(in_ref[pl.ds(at, group), :].astype(F32))
                rows = [(rows[0], rows[2]), (rows[1], rows[3]), (rows[4], pltpu.roll(rows[4], half, 1))]
                for tile, (re, im) in enumerate(rows):
                    rows_ref[tile, first, :] = re
                    rows_ref[tile, second, :] = im
        sign = jnp.where(lax.broadcasted_iota(jnp.int32, (LANES, step), 1) < near, 1.0, -1.0)
        for tile in range(3):
            keep = min(LANES, width - tile * LANES)
            here = slice(tile * LANES, tile * LANES + keep)
            for at in range(0, depth, step):
                turned = rows_ref[tile, at : at + step, :].T
                out_ref[0, here, at : at + step] = turned[:keep].astype(BF16)
                turned = pltpu.roll(turned, near, 1) * sign
                out_ref[1, here, at : at + step] = turned[:keep].astype(BF16)

    return pl.pallas_call(
        kernel,
        out_shape=jax.ShapeDtypeStruct((2, width, depth), BF16),
        in_specs=[SMEM, VMEM],
        out_specs=VMEM,
        scratch_shapes=[pltpu.VMEM((3, depth, LANES), F32)],
        compiler_params=LIMIT,
    )(here, slabs)


def multiply(half, left, right, total=None):
    depth, columns = right.shape
    width = left.shape[1]
    step = 256

    def kernel(half_ref, left_ref, right_ref, *refs):
        now = pl.ds(pl.multiple_of(pl.program_id(0) * step, step), step)
        for which in range(2):
            product = jnp.dot(left_ref[which], right_ref[:, now] if extra else right_ref[...], preferred_element_type=F32)
            if total is None:
                refs[0][which, :, now] = product
            else:
                refs[1][which] = refs[0][which, :, now] + product

    extra = [] if total is None else [total]
    return pl.pallas_call(
        kernel,
        grid_spec=pltpu.PrefetchScalarGridSpec(
            num_scalar_prefetch=1,
            grid=(columns // step,),
            in_specs=[pl.BlockSpec((2, width, depth), lambda j, half_ref: (0, 0, half_ref[0])), VMEM if extra else pl.BlockSpec((depth, step), lambda j, half_ref: (0, j))]
            + [VMEM] * len(extra),
            out_specs=pl.BlockSpec((2, width, step), lambda j, half_ref: (0, 0, j)) if extra else VMEM,
        ),
        out_shape=jax.ShapeDtypeStruct((2, width, columns), F32),
        compiler_params=SMALL,
        cost_estimate=pl.CostEstimate(
            flops=4 * width * depth * columns,
            bytes_accessed=2 * depth * (2 * width + columns) + 8 * width * columns,
            transcendentals=0,
        ),
    )(half, left, right, *extra)


def local(pair_elems, slot_pair, val_index, cond_index, val_energy, cond_energy):
    full = pair_elems.shape[2]
    n_row = lax.axis_size(ROW)
    n_col = lax.axis_size(COL)
    n_far = lax.axis_size("yh")
    n_z = lax.axis_size("z")
    row = lax.axis_index(ROW)
    core = lax.axis_index("core").astype(jnp.int32).reshape(1)
    position = (row * n_col + lax.axis_index(COL)).astype(jnp.int32).reshape(1)
    width = full // n_row
    span = 3 * LANES

    def place_of(block):
        z, far, side = block // (2 * n_far), block // 2 % n_far, block % 2
        return (far * 2 + side) * n_z + z

    right = split_right(pair_elems, n_col)
    right = lax.all_to_all(right, COL, split_axis=0, concat_axis=0, tiled=True)

    tables = (slot_pair, val_index, cond_index, val_energy, cond_energy)
    left = split_left(pair_elems, tables, position, n_row, span, place_of)
    left, right = lax.optimization_barrier((left, right))
    groups = [right]
    for step in range(1, n_far):
        groups.append(lax.ppermute(right, "yh", [(far, (far - step) % n_far) for far in range(n_far)]))
    left = lax.all_to_all(left, ("yh", "core", "z"), split_axis=0, concat_axis=0, tiled=True)
    left, groups = lax.optimization_barrier((left, groups))

    shift = lax.rem(row * width, LANES).astype(jnp.int32).reshape(1)
    left = pack_left(left, shift)
    left = jnp.broadcast_to(left[None], (n_col, *left.shape))
    right, left = lax.optimization_barrier((part_rows(groups), left))
    left = lax.all_to_all(left, COL, split_axis=0, concat_axis=0, tiled=True)
    right = lax.all_gather(right, "z", axis=0, tiled=True)
    here = lax.axis_index("yh").astype(jnp.int32).reshape(1)
    left = order_left(here, left.reshape(n_col * left.shape[1], LANES), n_row, n_col, n_far, width)
    right, left = lax.optimization_barrier((right, left))

    other = lax.ppermute(right, "core", [(0, 1), (1, 0)])
    total = multiply(core, left, right)
    return multiply(1 - core, left, other, total)


def solution(mesh):
    n_row, n_col = mesh.devices.shape
    torus = Mesh(mesh.devices.reshape(n_row // 8, 4, 2, 2, n_col // 2), (*ROW, *COL))
    in_specs = (P((*ROW, *COL), None, None), P(), P(), P(), P(), P())
    out_specs = P(None, ROW, COL)
    return jax.shard_map(local, mesh=torus, in_specs=in_specs, out_specs=out_specs, check_vma=False)
```
